768 devices in a mesh: dp: 12 (over z_lo, core), node: 64 (over y, x, z_hi).
Axes of the slice: x: 4, y: 8, z: 12 (z_hi: 2, z_lo: 6; z = z_hi * 6 + z_lo), core: 2. Of those that a mesh axis runs over, the one named last changes fastest.
Arguments:
- tokens: bfloat16 [24, 256, 8192], P('dp'), may hold values from -9 to 9, as said below
- context_gradient: bfloat16 [24, 256, 8192], P('dp', None, 'node'), may hold values from -6 to 6
- query_codes: bfloat16 [72, 128, 8192], P('dp', None, 'node'), may hold values from -1 to 1
- query_scale: bfloat16 [72, 8192], P('dp', 'node'), may hold values from 0.009887695 to 0.03857422
- keyval_codes: bfloat16 [72, 128, 2048], P('dp', None, 'node'), may hold values from -1 to 1
- keyval_scale: bfloat16 [72, 2048], P('dp', 'node'), may hold values from 0.009887695 to 0.03857422
Outputs:
- context: bfloat16 [24, 256, 8192], P('dp', None, 'node')
- grad_query: float32 [72, 128, 8192], P('dp', None, 'node')
- grad_keyval: float32 [72, 128, 2048], P('dp', None, 'node')
The draws below stay inside these ranges and needn't reach their ends.
Inputs may be any that keep to these rules, and one draw needn't show every extreme that they name: `tokens`: activations of the layer's input.
All inputs are finite; a program needn't handle non-finite values.
Results may differ from the reference program's by a relative error of at most 0.02.
The reference program's roundings to bfloat16 on the way count: a program that leaves them out, or rounds other values in their place, can miss the bound.
Values may be sent and summed in bfloat16 or wider, within the bound.
A program may use at most 32 MiB of HBM per device.

```python
import math
import jax
import jax.numpy as jnp
from jax import lax

D = 8192
HEAD_DIM = 128
GROUP = 8
BLOCK = 128
LENGTH = 256
SEQS = 2
HEADS = 64
SEQUENCES = 24
PADBLK = 72
PADROWS = 9216
KV_COLS = 2048
N_DP = 12


def draw_tokens(key, part):
    key = jax.random.fold_in(key, 11)
    base_key = jax.random.fold_in(key, 0)
    array_shape = (SEQUENCES, LENGTH, D)
    values = jnp.clip(jax.random.normal(base_key, array_shape, jnp.float32), -5.0, 5.0)
    return values.astype(jnp.bfloat16)


def level_of(own_key, shape, shards, low, largest):
    level, own = 1.0, jax.random.fold_in(own_key, 6)
    for axis_at, shards_of in shards:
        heights = jnp.exp(jax.random.uniform(jax.random.fold_in(own, axis_at), (shards_of,), jnp.float32, low / len(shards), largest / len(shards)))
        level = level * jnp.repeat(heights, shape[axis_at] // shards_of).reshape([-1 if axis == axis_at else 1 for axis in range(len(shape))])
    return level


def bell_draw(key, dims, width, most, pieces=(), kind=jnp.bfloat16):
    loudness = level_of(key, dims, pieces, -0.22, 0.18) if pieces else 1.0
    drawn = jax.random.normal(key, dims, jnp.float32) * width * loudness
    return jnp.minimum(jnp.maximum(drawn, -most), most).astype(kind)


def setup_inputs(seed: int = 0) -> dict:
    key_of = jax.random.split(jax.random.key(seed), 7)
    tokens = draw_tokens(jax.random.fold_in(key_of[6], 71), 0)
    context_gradient = bell_draw(key_of[1], (SEQUENCES, LENGTH, HEADS * HEAD_DIM), 1.0, 6.0, ((0, 12), (2, 64)))
    query_codes = jnp.clip(jax.random.uniform(key_of[2], (PADBLK, BLOCK, HEADS * HEAD_DIM), jnp.float32, -1.0, 1.0) * level_of(key_of[2], (PADBLK, BLOCK, HEADS * HEAD_DIM), ((0, 12), (2, 64)), -0.4, 0.0), -1.0, 1.0).astype(jnp.bfloat16)
    query_scale = jnp.clip(jnp.exp(math.log(0.03857422) - 1.3612931 * jax.random.uniform(key_of[3], (PADBLK, HEADS * HEAD_DIM), jnp.float32) ** level_of(key_of[3], (PADBLK, HEADS * HEAD_DIM), ((0, 12), (1, 64)), -0.2, 0.2)), 0.009887695, 0.03857422).astype(jnp.bfloat16)
    keyval_codes = jnp.clip(jax.random.uniform(key_of[4], (PADBLK, BLOCK, KV_COLS), jnp.float32, -1.0, 1.0) * level_of(key_of[4], (PADBLK, BLOCK, KV_COLS), ((0, 12), (2, 64)), -0.4, 0.0), -1.0, 1.0).astype(jnp.bfloat16)
    keyval_scale = jnp.clip(jnp.exp(math.log(0.03857422) - 1.3612931 * jax.random.uniform(key_of[5], (PADBLK, KV_COLS), jnp.float32) ** level_of(key_of[5], (PADBLK, KV_COLS), ((0, 12), (1, 64)), -0.2, 0.2)), 0.009887695, 0.03857422).astype(jnp.bfloat16)
    return dict(tokens=tokens, context_gradient=context_gradient, query_codes=query_codes, query_scale=query_scale, keyval_codes=keyval_codes, keyval_scale=keyval_scale)


highest = lax.Precision.HIGHEST

def rounded(tensor):
    return lax.optimization_barrier(tensor.astype(jnp.bfloat16)).astype(jnp.float32)

def dequantize(code_block, scales):
    block_list = D // BLOCK
    joined = code_block[:block_list].astype(jnp.float32) * scales[:block_list].astype(jnp.float32)[:, None, :]
    return joined.astype(jnp.bfloat16).reshape(D, code_block.shape[2])

def reference(tokens, context_gradient, query_codes, query_scale, keyval_codes, keyval_scale):
    w_query = dequantize(query_codes, query_scale)
    w_keyval = dequantize(keyval_codes, keyval_scale)
    part_width = HEAD_DIM // GROUP
    keyval_heads = HEADS // GROUP
    factor = 1.0 / math.sqrt(HEAD_DIM)
    tok_count = SEQS * LENGTH
    causal = lax.iota(jnp.int32, LENGTH)[:, None] >= lax.iota(jnp.int32, LENGTH)[None, :]

    def one_group(totals, inputs):
        tok_block, grad_block = inputs
        tok_rows = tok_block.reshape(tok_count, D)
        queries = rounded(jnp.dot(tok_rows, w_query, preferred_element_type=jnp.float32))
        keyval = rounded(jnp.dot(tok_rows, w_keyval, preferred_element_type=jnp.float32))
        layout = keyval.reshape(tok_count, keyval_heads, GROUP, 2, part_width)
        key_matrix_rows = layout[:, :, :, 0, :].reshape(SEQS, LENGTH, keyval_heads, HEAD_DIM)
        value_matrix_rows = layout[:, :, :, 1, :].reshape(SEQS, LENGTH, keyval_heads, HEAD_DIM)
        query_heads = queries.reshape(SEQS, LENGTH, keyval_heads, GROUP, HEAD_DIM)
        scores = jnp.einsum('slhgd,smhd->shglm', query_heads, key_matrix_rows, precision=highest) * factor
        scores = jnp.where(causal, scores, -jnp.inf)
        shifted = jnp.exp(scores - lax.optimization_barrier(jnp.max(scores, axis=-1, keepdims=True)))
        attend = shifted / lax.optimization_barrier(jnp.sum(shifted, axis=-1, keepdims=True))
        attend_lower_half = rounded(attend)
        mixed = jnp.einsum('shglm,smhd->slhgd', attend_lower_half, value_matrix_rows, precision=highest)
        outputs = mixed.astype(jnp.bfloat16).reshape(SEQS, LENGTH, HEADS * HEAD_DIM)
        cotangent = grad_block.astype(jnp.float32).reshape(SEQS, LENGTH, keyval_heads, GROUP, HEAD_DIM)
        back_attend = jnp.einsum('slhgd,smhd->shglm', cotangent, value_matrix_rows, precision=highest)
        center = lax.optimization_barrier(jnp.sum(back_attend * attend, axis=-1, keepdims=True))
        scores_backward = rounded(attend * (back_attend - center) * factor)
        back_query = jnp.einsum('shglm,smhd->slhgd', scores_backward, key_matrix_rows, precision=highest)
        back_query = back_query.astype(jnp.bfloat16).reshape(tok_count, HEADS * HEAD_DIM)
        back_key = jnp.einsum('shglm,slhgd->smhd', scores_backward, query_heads, precision=highest)
        back_value = jnp.einsum('shglm,slhgd->smhd', attend_lower_half, cotangent, precision=highest)
        back_keyval = jnp.stack([back_key.reshape(tok_count, keyval_heads, GROUP, part_width), back_value.reshape(tok_count, keyval_heads, GROUP, part_width)], axis=3)
        back_keyval = back_keyval.reshape(tok_count, 2 * HEADS * part_width).astype(jnp.bfloat16)
        part_query = rounded(jnp.dot(tok_rows.T, back_query, preferred_element_type=jnp.float32))
        part_keyval = rounded(jnp.dot(tok_rows.T, back_keyval, preferred_element_type=jnp.float32))
        return ((totals[0] + part_query, totals[1] + part_keyval), outputs)
    start_totals = (jnp.zeros((D, HEADS * HEAD_DIM), jnp.float32), jnp.zeros((D, 2 * HEADS * part_width), jnp.float32))
    tok_groups = tokens.reshape(N_DP, SEQS, LENGTH, D)
    grad_groups = context_gradient.reshape(N_DP, SEQS, LENGTH, HEADS * HEAD_DIM)
    totals, outputs = lax.scan(one_group, start_totals, (tok_groups, grad_groups))
    context = outputs.reshape(SEQS * N_DP, LENGTH, HEADS * HEAD_DIM)
    extra = PADROWS - D
    grad_query = jnp.pad(totals[0], ((0, extra), (0, 0))).reshape(PADBLK, BLOCK, HEADS * HEAD_DIM)
    grad_keyval = jnp.pad(totals[1], ((0, extra), (0, 0))).reshape(PADBLK, BLOCK, 2 * HEADS * part_width)
    return (context, grad_query, grad_keyval)
```

```python
import functools
import math

import jax
import jax.numpy as jnp
from jax import lax
from jax.experimental import pallas as pl
from jax.experimental.pallas import tpu as pltpu
from jax.sharding import PartitionSpec as P

MESH = pl.DeviceIdType.MESH
F32 = jnp.float32
BF16 = jnp.bfloat16
CHIPS = 6
LAST = CHIPS - 1
PIECES = 3
STEP = 256
GROUP = 8


def dot(a, b, dim_a=1, dim_b=0):
    return lax.dot_general(a, b, (((dim_a,), (dim_b,)), ((), ())), preferred_element_type=F32)


def kernel(
    tok_hbm, grad_ref, qc_ref, qs_ref, kc_ref, ks_ref,
    ctx_ref, gq_ref, gkv_ref,
    x_all, wq, wkv, kv, q_acc, kv_acc, back, kv_part, kv_low, kv_in, pair_sum, z_out, z_in,
    own_part, sib_out, sib_in, run_out, run_in,
    x_sem, ag_r, ag_s, rs_r, rs_s, sib_r, sib_s, kvz, kvx_s, kvx_r, dkz, dkx_s, dkx_r,
):
    dp = lax.axis_index("dp")
    node = lax.axis_index("node")
    chip = dp // 2
    core = dp % 2
    member = node % GROUP
    z_hi = member % 2
    x_at = member // 2
    sibling = {"dp": 2 * chip + 1 - core}
    z_twin = {"node": node + 1 - 2 * z_hi}
    tok_count = grad_ref.shape[0]
    length = 256

    def x_mate(delta):
        return {"node": node - member + ((x_at + delta) % 4) * 2 + z_hi}

    def place(way):
        return chip if way == 0 else LAST - chip

    def ahead(way):
        return {"dp": dp + 2 if way == 0 else dp - 2}

    def chip_of(way, position):
        return position if way == 0 else LAST - position

    def remote(src, dst, s_sem, r_sem, to):
        return pltpu.make_async_remote_copy(
            src_ref=src, dst_ref=dst, send_sem=s_sem, recv_sem=r_sem, device_id=to, device_id_type=MESH
        )

    loaded = x_all.at[pl.ds(0, 32)]
    x_copy = pltpu.make_async_copy(loaded, loaded, x_sem)
    for i in range(32):
        pltpu.make_async_copy(tok_hbm.at[:, pl.ds(i * STEP, STEP)], x_all.at[i], x_sem).start()
    x_all[32:36] = jnp.zeros((4, tok_count, STEP), BF16)

    for b in range(6):
        rows = pl.ds(b * 128, 128)
        wq[dp, rows, :] = (qc_ref[b].astype(F32) * qs_ref[b : b + 1, :].astype(F32)).astype(BF16)
        wkv[dp, :, rows] = (kc_ref[b].astype(F32) * ks_ref[:, b : b + 1].astype(F32)).astype(BF16)

    barrier = pltpu.get_barrier_semaphore()
    for to in (sibling, z_twin, x_mate(1), x_mate(2), x_mate(3)):
        pl.semaphore_signal(barrier, inc=1, device_id=to, device_id_type=MESH)
    for way in range(2):
        @pl.when(place(way) < LAST)
        def _():
            pl.semaphore_signal(barrier, inc=1, device_id=ahead(way), device_id_type=MESH)
    pl.semaphore_wait(barrier, 7 - (chip == 0).astype(jnp.int32) - (chip == LAST).astype(jnp.int32))

    def chunk(owner, piece):
        if piece == 0:
            return wkv.at[owner]
        return wq.at[owner, pl.ds((piece - 1) * STEP, STEP), :]

    def ag_copy(src_chip, piece, to, s_sem):
        owner = 2 * src_chip + core
        part = chunk(owner, piece)
        return remote(part, part, s_sem, ag_r.at[owner, piece], to)

    def ag_wait(owner, piece):
        part = chunk(owner, piece)
        remote(part, part, ag_s.at[2, 0, piece], ag_r.at[owner, piece], sibling).wait_recv()

    def ag_send(src_chip, piece, only=(0, 1)):
        for way in only:
            @pl.when(place(way) < LAST)
            def _():
                ag_copy(src_chip, piece, ahead(way), ag_s.at[way, src_chip, piece]).start()
        ag_copy(src_chip, piece, sibling, ag_s.at[2, src_chip, piece]).start()

    def use_kv(owner):
        total = kv_acc[...]
        for p in range(PIECES):
            total += dot(wkv[owner, :, p * STEP : (p + 1) * STEP], x_all[owner * PIECES + p], 1, 1)
        kv_acc[...] = total

    def use_q(owner, p):
        q_acc[...] += dot(x_all[owner * PIECES + p], wq[owner, p * STEP : (p + 1) * STEP, :])

    def each_source(distance, body):
        for way in range(2):
            src = chip_of(way, place(way) - distance)
            @pl.when(place(way) >= distance)
            def _():
                body(way, src)

    def take(src, piece):
        other = 2 * src + 1 - core
        ag_wait(other, piece)
        if piece == 0:
            use_kv(2 * src + core)
            use_kv(other)
        else:
            use_q(2 * src + core, piece - 1)
            use_q(other, piece - 1)

    q_acc[...] = jnp.zeros_like(q_acc)
    kv_acc[...] = jnp.zeros_like(kv_acc)
    ag_send(chip, 0)
    ag_send(chip, 1)
    x_copy.wait()

    def pass_on(distance, piece):
        def body(way, src):
            ag_wait(2 * src + core, piece)
            ag_send(src, piece, (way,))
        each_source(distance, body)

    pass_on(1, 0)
    ag_send(chip, 2)
    take(chip, 0)
    pass_on(2, 0)
    ag_send(chip, 3)
    each_source(1, lambda way, src: take(src, 0))

    def kv_step(d, carry):
        pass_on(d, 0)
        each_source(d - 1, lambda way, src: take(src, 0))
        return carry

    lax.fori_loop(3, CHIPS, kv_step, 0)
    each_source(LAST, lambda way, src: take(src, 0))
    kv[member] = kv_acc[...].astype(BF16).reshape(2, 16, tok_count)
    z_copy = remote(kv.at[member], kv.at[member], kvz.at[0], kvz.at[1], z_twin)
    z_copy.start()

    def q_step(d, carry):
        for p in range(PIECES):
            pass_on(d, p + 1)

            @pl.when(d == 1)
            def _():
                take(chip, p + 1)

            @pl.when(d > 1)
            def _():
                each_source(d - 1, lambda way, src: take(src, p + 1))
        return carry

    lax.fori_loop(1, 2, q_step, 0)

    pair = pl.ds(x_at * 2, 2)
    z_copy.wait()
    kv_copies = []
    for delta in (1, 2, 3):
        copy = remote(kv.at[pair], kv.at[pair], kvx_s.at[delta - 1], kvx_r.at[delta - 1], x_mate(delta))
        copy.start()
        kv_copies.append(copy)

    lax.fori_loop(2, CHIPS, q_step, 0)
    for p in range(PIECES):
        each_source(LAST, lambda way, src: take(src, p + 1))
    for copy in kv_copies:
        copy.wait()

    factor = 1.0 / math.sqrt(128)
    keys = kv[:, 0].reshape(128, tok_count)
    values = kv[:, 1].reshape(128, tok_count)
    seen = lax.broadcasted_iota(jnp.int32, (length, length), 0) >= lax.broadcasted_iota(
        jnp.int32, (length, length), 1
    )
    for s in range(tok_count // length):
        at = slice(s * length, (s + 1) * length)
        queries = q_acc[at, :].astype(BF16)
        grad = grad_ref[at, :]
        key_t, value_t = keys[:, at], values[:, at]
        scores = jnp.where(seen, dot(queries, key_t) * factor, -jnp.inf)
        shifted = jnp.exp(scores - jnp.max(scores, axis=1, keepdims=True))
        attend = shifted / jnp.sum(shifted, axis=1, keepdims=True)
        low = attend.astype(BF16)
        back_attend = dot(grad, value_t)
        center = jnp.sum(back_attend * attend, axis=1, keepdims=True)
        back_scores = (attend * (back_attend - center) * factor).astype(BF16)
        kv_part[:, 0, :, at] = dot(queries, back_scores, 0, 0).reshape(GROUP, 16, length)
        kv_part[:, 1, :, at] = dot(grad, low, 0, 0).reshape(GROUP, 16, length)
        back[0:128, at] = dot(key_t, back_scores, 1, 1).astype(BF16)
        ctx_ref[at, :] = dot(low, value_t, 1, 1).astype(BF16)
    kv_low[...] = kv_part[...].astype(BF16)
    dk_copies = []
    for delta in (1, 2, 3):
        theirs = pl.ds(((x_at + delta) % 4) * 2, 2)
        copy = remote(kv_low.at[theirs], kv_in.at[delta - 1], dkx_s.at[delta - 1], dkx_r.at[delta - 1], x_mate(delta))
        copy.start()
        dk_copies.append(copy)

    def sib_copy(dest, piece):
        if piece < PIECES:
            src, dst = sib_out.at[dest, piece, pl.ds(0, 128)], sib_in.at[dest, piece, pl.ds(0, 128)]
        else:
            src, dst = sib_out.at[dest, :, pl.ds(128, 32)], sib_in.at[dest, :, pl.ds(128, 32)]
        return remote(src, dst, sib_s.at[dest, piece], sib_r.at[dest, piece], sibling)

    def run_copy(way, dest, piece):
        if piece < PIECES:
            src, dst = run_out.at[dest, piece, pl.ds(0, 128)], run_in.at[way, dest, piece, pl.ds(0, 128)]
        else:
            src, dst = run_out.at[dest, :, pl.ds(128, 32)], run_in.at[way, dest, :, pl.ds(128, 32)]
        return remote(src, dst, rs_s.at[dest, piece], rs_r.at[way, dest, piece], ahead(way))

    def terms(dest, rows, piece):
        theirs = (2 * dest + 1 - core) * PIECES
        ours = (2 * dest + core) * PIECES
        pieces = (piece,) if piece < PIECES else range(PIECES)
        for p in pieces:
            sib_out[dest, p, rows, :] = dot(back[rows, :], x_all[theirs + p]).astype(BF16)
        sib_copy(dest, piece).start()
        for p in pieces:
            own_part[dest, p, rows, :] = dot(back[rows, :], x_all[ours + p]).astype(BF16)

    q_rows, kv_rows = slice(0, 128), slice(128, 160)

    def q_terms(dest):
        for p in range(PIECES):
            terms(dest, q_rows, p)

    def each_dest(time, body):
        for way in range(2):
            dest = chip_of(way, LAST - time + place(way))
            @pl.when(time >= place(way))
            def _():
                body(way, dest)

    def combine(way, dest, piece):
        rows = q_rows if piece < PIECES else kv_rows
        pieces = (piece,) if piece < PIECES else range(PIECES)
        sib_copy(dest, piece).wait_recv()

        @pl.when(place(way) > 0)
        def _():
            run_copy(way, dest, piece).wait_recv()
            for p in pieces:
                run_out[dest, p, rows, :] = (
                    own_part[dest, p, rows, :].astype(F32)
                    + sib_in[dest, p, rows, :].astype(F32)
                    + run_in[way, dest, p, rows, :].astype(F32)
                ).astype(BF16)

        @pl.when(place(way) == 0)
        def _():
            for p in pieces:
                run_out[dest, p, rows, :] = (
                    own_part[dest, p, rows, :].astype(F32) + sib_in[dest, p, rows, :].astype(F32)
                ).astype(BF16)

        run_copy(way, dest, piece).start()

    def q_time(time, carry):
        @pl.when(time < LAST - 1)
        def _():
            each_dest(time + 1, lambda way, dest: q_terms(dest))

        for p in range(PIECES):
            each_dest(time, lambda way, dest: combine(way, dest, p))
        return carry

    each_dest(0, lambda way, dest: q_terms(dest))
    lax.fori_loop(0, 2, q_time, 0)

    for copy in dk_copies:
        copy.wait()
    pair_sum[...] = (
        kv_part[pair]
        + kv_in[0].astype(F32)
        + kv_in[1].astype(F32)
        + kv_in[2].astype(F32)
    )
    z_out[...] = pair_sum[1 - z_hi].astype(BF16)
    dz_copy = remote(z_out, z_in, dkz.at[0], dkz.at[1], z_twin)
    dz_copy.start()
    lax.fori_loop(2, 3, q_time, 0)
    dz_copy.wait()
    back[128:160, :] = (pair_sum[z_hi] + z_in[...].astype(F32)).astype(BF16).reshape(32, tok_count)

    def kv_terms(dest, carry):
        terms(dest, kv_rows, PIECES)
        return carry

    lax.fori_loop(0, CHIPS, kv_terms, 0)

    def kv_time(time, carry):
        each_dest(time, lambda way, dest: combine(way, dest, PIECES))
        return carry

    def both(time, carry):
        kv_time(time - 3, 0)
        return q_time(time, carry)

    lax.fori_loop(3, CHIPS - 1, both, 0)
    q_terms(chip)
    lax.fori_loop(2, CHIPS - 1, kv_time, 0)

    for piece in range(PIECES + 1):
        rows = q_rows if piece < PIECES else kv_rows
        pieces = (piece,) if piece < PIECES else range(PIECES)
        sib_copy(chip, piece).wait_recv()
        for p in pieces:
            run_sum = own_part[chip, p, rows, :].astype(F32) + sib_in[chip, p, rows, :].astype(F32)
            if piece < PIECES:
                gq_ref[2 * p : 2 * p + 2] = run_sum.T.reshape(2, 128, 128)
            else:
                gkv_ref[2 * p] = run_sum[:, 0:128]
                gkv_ref[2 * p + 1] = run_sum[:, 128:256]
        for way in range(2):
            @pl.when(place(way) > 0)
            def _():
                run_copy(way, chip, piece).wait_recv()
                for p in pieces:
                    more = run_in[way, chip, p, rows, :].astype(F32)
                    if piece < PIECES:
                        gq_ref[2 * p : 2 * p + 2] += more.T.reshape(2, 128, 128)
                    else:
                        gkv_ref[2 * p] += more[:, 0:128]
                        gkv_ref[2 * p + 1] += more[:, 128:256]

    def drain(at, carry):
        for piece in range(PIECES + 1):
            for way in range(2):
                @pl.when((place(way) < LAST) & ((at <= chip) if way == 0 else (at >= chip)))
                def _():
                    ag_copy(at, piece, sibling, ag_s.at[way, at, piece]).wait_send()

                @pl.when((at > chip) if way == 0 else (at < chip))
                def _():
                    run_copy(way, at, piece).wait_send()
            ag_copy(at, piece, sibling, ag_s.at[2, at, piece]).wait_send()
            sib_copy(at, piece).wait_send()
        return carry

    lax.fori_loop(0, CHIPS, drain, 0)


def per_device(tokens, context_gradient, query_codes, query_scale, keyval_codes, keyval_scale):
    seq_count, length, width = tokens.shape
    tok_count = seq_count * length
    dma = pltpu.SemaphoreType.DMA
    vmem = pl.BlockSpec(memory_space=pltpu.VMEM)
    out = pl.pallas_call(
        kernel,
        out_shape=(
            jax.ShapeDtypeStruct((tok_count, 128), BF16),
            jax.ShapeDtypeStruct((6, 128, 128), F32),
            jax.ShapeDtypeStruct((6, 32, 128), F32),
        ),
        in_specs=[pl.BlockSpec(memory_space=pl.ANY)] + [vmem] * 5,
        out_specs=(vmem, vmem, vmem),
        scratch_shapes=[
            pltpu.VMEM((36, tok_count, STEP), BF16),
            pltpu.VMEM((12, 768, 128), BF16),
            pltpu.VMEM((12, 32, 768), BF16),
            pltpu.VMEM((GROUP, 2, 16, tok_count), BF16),
            pltpu.VMEM((tok_count, 128), F32),
            pltpu.VMEM((32, tok_count), F32),
            pltpu.VMEM((160, tok_count), BF16),
            pltpu.VMEM((GROUP, 2, 16, tok_count), F32),
            pltpu.VMEM((GROUP, 2, 16, tok_count), BF16),
            pltpu.VMEM((3, 2, 2, 16, tok_count), BF16),
            pltpu.VMEM((2, 2, 16, tok_count), F32),
            pltpu.VMEM((2, 16, tok_count), BF16),
            pltpu.VMEM((2, 16, tok_count), BF16),
            pltpu.VMEM((CHIPS, PIECES, 160, STEP), BF16),
            pltpu.VMEM((CHIPS, PIECES, 160, STEP), BF16),
            pltpu.VMEM((CHIPS, PIECES, 160, STEP), BF16),
            pltpu.VMEM((CHIPS, PIECES, 160, STEP), BF16),
            pltpu.VMEM((2, CHIPS, PIECES, 160, STEP), BF16),
            dma(()),
            dma((12, PIECES + 1)),
            dma((3, CHIPS, PIECES + 1)),
            dma((2, CHIPS, PIECES + 1)),
            dma((CHIPS, PIECES + 1)),
            dma((CHIPS, PIECES + 1)),
            dma((CHIPS, PIECES + 1)),
            dma((2,)),
            dma((3,)),
            dma((3,)),
            dma((2,)),
            dma((3,)),
            dma((3,)),
        ],
        compiler_params=pltpu.CompilerParams(
            collective_id=0, has_side_effects=True, vmem_limit_bytes=48 * 1024 * 1024
        ),
    )(
        tokens.reshape(tok_count, width),
        context_gradient.reshape(tok_count, 128),
        query_codes,
        query_scale,
        keyval_codes.transpose(0, 2, 1),
        keyval_scale.T,
    )
    return out[0].reshape(context_gradient.shape), out[1], out[2].transpose(0, 2, 1)


def solution(mesh):
    return jax.shard_map(
        per_device,
        mesh=mesh,
        in_specs=(
            P("dp", None, None),
            P("dp", None, "node"),
            P("dp", None, "node"),
            P("dp", "node"),
            P("dp", None, "node"),
            P("dp", "node"),
        ),
        out_specs=(P("dp", None, "node"), P("dp", None, "node"), P("dp", None, "node")),
        check_vma=False,
    )
```

```python
import functools
import math

import jax
import jax.numpy as jnp
from jax import lax
from jax.experimental import pallas as pl
from jax.experimental.pallas import tpu as pltpu
from jax.sharding import PartitionSpec as P

MESH = pl.DeviceIdType.MESH
F32 = jnp.float32
BF16 = jnp.bfloat16
CHIPS = 6
LAST = CHIPS - 1
PIECES = 3
STEP = 256
GROUP = 8
VLIM = 60


def dot(a, b, dim_a=1, dim_b=0):
    return lax.dot_general(a, b, (((dim_a,), (dim_b,)), ((), ())), preferred_element_type=F32)


def kernel(
    tok_hbm, grad_hbm, qc_hbm, qs_hbm, kc_hbm, ks_hbm,
    ctx_ref, gq_ref, gkv_ref,
    grad_ref, qc_ref, qs_ref, kc_ref, ks_ref, x_all, wq, wkv, kv, q_acc, kv_acc, back, kv_part, kv_low, kv_in, pair_sum, z_out, z_in,
    grad_values, q_low, attend_low, scores_low, own_part, sib_out, sib_in, run_out, run_in,
    in_sem, x_sem, ag_r, ag_s, rs_r, rs_s, sib_r, sib_s, kvz, kvx_s, kvx_r, dkz, dkx_s, dkx_r,
):
    dp = lax.axis_index("dp")
    node = lax.axis_index("node")
    chip = dp // 2
    core = dp % 2
    member = node % GROUP
    z_hi = member % 2
    x_at = member // 2
    sibling = {"dp": 2 * chip + 1 - core}
    z_twin = {"node": node + 1 - 2 * z_hi}
    tok_count = grad_ref.shape[0]
    length = scores_low.shape[1]

    def x_mate(delta):
        return {"node": node - member + ((x_at + delta) % 4) * 2 + z_hi}

    def place(way):
        return chip if way == 0 else LAST - chip

    def ahead(way):
        return {"dp": dp + 2 if way == 0 else dp - 2}

    def chip_of(way, position):
        return position if way == 0 else LAST - position

    def remote(src, dst, s_sem, r_sem, to):
        return pltpu.make_async_remote_copy(
            src_ref=src, dst_ref=dst, send_sem=s_sem, recv_sem=r_sem, device_id=to, device_id_type=MESH
        )

    small = [
        pltpu.make_async_copy(src, dst, in_sem.at[i])
        for i, (src, dst) in enumerate(
            ((kc_hbm, kc_ref), (ks_hbm, ks_ref), (qc_hbm, qc_ref), (qs_hbm, qs_ref), (grad_hbm, grad_ref))
        )
    ]
    for copy in small:
        copy.start()
    loaded = x_all.at[pl.ds(0, 32)]
    x_copy = pltpu.make_async_copy(loaded, loaded, x_sem)
    for i in range(32):
        pltpu.make_async_copy(tok_hbm.at[:, pl.ds(i * STEP, STEP)], x_all.at[i], x_sem).start()

    barrier = pltpu.get_barrier_semaphore()
    for to in (sibling, z_twin, x_mate(1), x_mate(2), x_mate(3)):
        pl.semaphore_signal(barrier, inc=1, device_id=to, device_id_type=MESH)
    for way in range(2):
        @pl.when(place(way) < LAST)
        def _():
            pl.semaphore_signal(barrier, inc=1, device_id=ahead(way), device_id_type=MESH)

    for copy in small:
        copy.wait()
    diagonal = lax.broadcasted_iota(jnp.int32, (32, 32), 0) == lax.broadcasted_iota(jnp.int32, (32, 32), 1)
    for b in range(6):
        rows = pl.ds(b * 128, 128)
        scale = jnp.where(diagonal, ks_ref[b : b + 1, :].astype(F32), 0.0).sum(axis=1, keepdims=True)
        wkv[dp, :, rows] = (kc_ref[b].astype(F32) * scale).astype(BF16)
    for b in range(6):
        rows = pl.ds(b * 128, 128)
        wq[dp, rows, :] = (qc_ref[b].astype(F32) * qs_ref[b : b + 1, :].astype(F32)).astype(BF16)
    pl.semaphore_wait(barrier, 7 - (chip == 0).astype(jnp.int32) - (chip == LAST).astype(jnp.int32))

    def chunk(owner, piece):
        if isinstance(piece, int) and piece == 0:
            return wkv.at[owner]
        return wq.at[owner, pl.ds(pl.multiple_of((piece - 1) * STEP, STEP), STEP), :]

    def ag_copy(src_chip, piece, to, s_sem):
        owner = 2 * src_chip + core
        part = chunk(owner, piece)
        return remote(part, part, s_sem, ag_r.at[owner, piece], to)

    def ag_wait(owner, piece):
        part = chunk(owner, piece)
        remote(part, part, ag_s.at[2, 0, piece], ag_r.at[owner, piece], sibling).wait_recv()

    def ag_send(src_chip, piece, only=(0, 1)):
        for way in only:
            @pl.when(place(way) < LAST)
            def _():
                ag_copy(src_chip, piece, ahead(way), ag_s.at[way, src_chip, piece]).start()
        ag_copy(src_chip, piece, sibling, ag_s.at[2, src_chip, piece]).start()

    def use_kv(owner):
        total = kv_acc[...]
        for p in range(PIECES):
            total += dot(wkv[owner, :, p * STEP : (p + 1) * STEP], x_all[owner * PIECES + p], 1, 1)
        kv_acc[...] = total

    def use_q(owner, other, p):
        q_acc[...] += dot(x_all[owner * PIECES + p], wq[owner, p * STEP : (p + 1) * STEP, :]) + dot(
            x_all[other * PIECES + p], wq[other, p * STEP : (p + 1) * STEP, :]
        )

    def each_source(distance, body):
        for way in range(2):
            src = chip_of(way, place(way) - distance)
            @pl.when(place(way) >= distance)
            def _():
                body(way, src)

    def take(src, piece):
        other = 2 * src + 1 - core
        ag_wait(other, piece)
        if piece == 0:
            use_kv(2 * src + core)
            use_kv(other)
        else:
            use_q(2 * src + core, other, piece - 1)

    q_acc[...] = jnp.zeros_like(q_acc)
    kv_acc[...] = jnp.zeros_like(kv_acc)
    def pass_on(distance, piece):
        def body(way, src):
            ag_wait(2 * src + core, piece)
            ag_send(src, piece, (way,))
        each_source(distance, body)

    ag_send(chip, 0)
    ag_send(chip, 1)
    pass_on(1, 0)
    ag_send(chip, 2)
    pass_on(2, 0)
    ag_send(chip, 3)
    x_all[32:36] = jnp.zeros((4, tok_count, STEP), BF16)
    x_copy.wait()
    take(chip, 0)

    def kv_step(d, carry):
        pass_on(d, 0)
        pass_on(1, d - 2)
        each_source(d - 2, lambda way, src: take(src, 0))
        return carry

    lax.fori_loop(3, CHIPS, kv_step, 0)
    pass_on(2, 1)
    each_source(LAST - 1, lambda way, src: take(src, 0))
    each_source(LAST, lambda way, src: take(src, 0))
    kv[member] = kv_acc[...].astype(BF16).reshape(2, 16, tok_count)
    z_copy = remote(kv.at[member], kv.at[member], kvz.at[0], kvz.at[1], z_twin)
    z_copy.start()
    pass_on(2, 2)
    pass_on(2, 3)
    for p in range(PIECES):
        take(chip, p + 1)

    def q_step(d, carry):
        for p in range(PIECES):
            pass_on(d, p + 1)
            each_source(d - 2, lambda way, src: take(src, p + 1))
        return carry

    lax.fori_loop(3, 4, q_step, 0)

    pair = pl.ds(x_at * 2, 2)
    z_copy.wait()
    kv_copies = []
    for delta in (1, 2, 3):
        copy = remote(kv.at[pair], kv.at[pair], kvx_s.at[delta - 1], kvx_r.at[delta - 1], x_mate(delta))
        copy.start()
        kv_copies.append(copy)

    lax.fori_loop(4, CHIPS, q_step, 0)
    for p in range(PIECES):
        each_source(LAST - 1, lambda way, src: take(src, p + 1))
    for copy in kv_copies:
        copy.wait()
    for s in range(tok_count // length):
        at = slice(s * length, (s + 1) * length)
        grad_values[at, :] = dot(grad_ref[at, :], kv[:, 1, :, at].reshape(128, length))
    for p in range(PIECES):
        each_source(LAST, lambda way, src: take(src, p + 1))

    factor = 1.0 / math.sqrt(128)
    keys = kv[:, 0].reshape(128, tok_count)
    values = kv[:, 1].reshape(128, tok_count)
    seen = lax.broadcasted_iota(jnp.int32, (length, length), 0) >= lax.broadcasted_iota(
        jnp.int32, (length, length), 1
    )
    for s in range(tok_count // length):
        at = slice(s * length, (s + 1) * length)
        queries = q_acc[at, :].astype(BF16)
        q_low[at, :] = queries
        scores = jnp.where(seen, dot(queries, keys[:, at]) * factor, -jnp.inf)
        shifted = jnp.exp(scores - jnp.max(scores, axis=1, keepdims=True))
        attend = shifted / jnp.sum(shifted, axis=1, keepdims=True)
        attend_low[at, :] = attend.astype(BF16)
        back_attend = grad_values[at, :]
        center = jnp.sum(back_attend * attend, axis=1, keepdims=True)
        back_scores = (attend * (back_attend - center) * factor).astype(BF16)
        scores_low[at, :] = back_scores
        back[0:128, at] = dot(keys[:, at], back_scores, 1, 1).astype(BF16)

    def rest_of_attention():
        for s in range(tok_count // length):
            at = slice(s * length, (s + 1) * length)
            kv_part[:, 0, :, at] = dot(q_low[at, :], scores_low[at, :], 0, 0).reshape(GROUP, 16, length)
            kv_part[:, 1, :, at] = dot(grad_ref[at, :], attend_low[at, :], 0, 0).reshape(GROUP, 16, length)
        kv_low[...] = kv_part[...].astype(BF16)
        for copy in dk_copies:
            copy.start()
        for s in range(tok_count // length):
            at = slice(s * length, (s + 1) * length)
            ctx_ref[at, :] = dot(attend_low[at, :], values[:, at], 1, 1).astype(BF16)

    dk_copies = []
    for delta in (1, 2, 3):
        theirs = pl.ds(((x_at + delta) % 4) * 2, 2)
        dk_copies.append(
            remote(kv_low.at[theirs], kv_in.at[delta - 1], dkx_s.at[delta - 1], dkx_r.at[delta - 1], x_mate(delta))
        )

    def sib_copy(dest, piece):
        if piece < PIECES:
            src, dst = sib_out.at[dest, piece, pl.ds(0, 128)], sib_in.at[dest, piece, pl.ds(0, 128)]
        else:
            src, dst = sib_out.at[dest, :, pl.ds(128, 32)], sib_in.at[dest, :, pl.ds(128, 32)]
        return remote(src, dst, sib_s.at[dest, piece], sib_r.at[dest, piece], sibling)

    def run_copy(way, dest, piece):
        if piece < PIECES:
            src, dst = run_out.at[dest, piece, pl.ds(0, 128)], run_in.at[way, dest, piece, pl.ds(0, 128)]
        else:
            src, dst = run_out.at[dest, :, pl.ds(128, 32)], run_in.at[way, dest, :, pl.ds(128, 32)]
        return remote(src, dst, rs_s.at[dest, piece], rs_r.at[way, dest, piece], ahead(way))

    q_rows, kv_rows = slice(0, 128), slice(128, 160)

    def terms(dest, rows):
        theirs = (2 * dest + 1 - core) * PIECES
        ours = (2 * dest + core) * PIECES
        low = back[rows, :]
        sib = [dot(low, x_all[theirs + p]).astype(BF16) for p in range(PIECES)]
        own = [dot(low, x_all[ours + p]).astype(BF16) for p in range(PIECES)]
        for p in range(PIECES):
            sib_out[dest, p, rows, :] = sib[p]
        for piece in range(PIECES) if rows == q_rows else (PIECES,):
            sib_copy(dest, piece).start()
        for p in range(PIECES):
            own_part[dest, p, rows, :] = own[p]

    def each_dest(time, body):
        for way in range(2):
            dest = chip_of(way, LAST - time + place(way))
            @pl.when(time >= place(way))
            def _():
                body(way, dest)

    def combine(way, dest, piece):
        rows = q_rows if piece < PIECES else kv_rows
        pieces = (piece,) if piece < PIECES else range(PIECES)
        sib_copy(dest, piece).wait_recv()

        @pl.when(place(way) > 0)
        def _():
            run_copy(way, dest, piece).wait_recv()
            for p in pieces:
                run_out[dest, p, rows, :] = (
                    own_part[dest, p, rows, :].astype(F32)
                    + sib_in[dest, p, rows, :].astype(F32)
                    + run_in[way, dest, p, rows, :].astype(F32)
                ).astype(BF16)

        @pl.when(place(way) == 0)
        def _():
            for p in pieces:
                run_out[dest, p, rows, :] = (
                    own_part[dest, p, rows, :].astype(F32) + sib_in[dest, p, rows, :].astype(F32)
                ).astype(BF16)

        run_copy(way, dest, piece).start()

    def q_terms(time):
        each_dest(time, lambda way, dest: terms(dest, q_rows))

    def kv_terms(time):
        each_dest(time, lambda way, dest: terms(dest, kv_rows))

    def q_combine(time, p):
        each_dest(time, lambda way, dest: combine(way, dest, p))

    def kv_combine(time):
        each_dest(time, lambda way, dest: combine(way, dest, PIECES))

    def q_time(time):
        q_terms(time)
        for p in range(PIECES):
            q_combine(time, p)

    q_time(0)
    rest_of_attention()
    q_time(1)

    for copy in dk_copies:
        copy.wait()
    pair_sum[...] = (
        kv_part[pair] + kv_in[0].astype(F32) + kv_in[1].astype(F32) + kv_in[2].astype(F32)
    )
    z_out[...] = pair_sum[1 - z_hi].astype(BF16)
    dz_copy = remote(z_out, z_in, dkz.at[0], dkz.at[1], z_twin)
    dz_copy.start()
    q_time(2)
    q_terms(3)
    q_combine(3, 0)
    q_combine(3, 1)
    dz_copy.wait()
    back[128:160, :] = (pair_sum[z_hi] + z_in[...].astype(F32)).astype(BF16).reshape(32, tok_count)
    kv_terms(0)
    kv_terms(1)
    kv_combine(0)
    q_combine(3, 2)
    kv_terms(2)
    kv_combine(1)
    q_terms(4)
    q_combine(4, 0)
    kv_terms(3)
    kv_combine(2)
    q_combine(4, 1)
    kv_terms(4)
    kv_combine(3)
    terms(chip, q_rows)
    q_combine(4, 2)
    terms(chip, kv_rows)
    kv_combine(4)

    for piece in range(PIECES + 1):
        rows = q_rows if piece < PIECES else kv_rows
        pieces = (piece,) if piece < PIECES else range(PIECES)
        sib_copy(chip, piece).wait_recv()
        for p in pieces:
            run_sum = own_part[chip, p, rows, :].astype(F32) + sib_in[chip, p, rows, :].astype(F32)
            if piece < PIECES:
                gq_ref[2 * p : 2 * p + 2] = run_sum.T.reshape(2, 128, 128)
            else:
                gkv_ref[2 * p] = run_sum[:, 0:128]
                gkv_ref[2 * p + 1] = run_sum[:, 128:256]
        for way in range(2):
            @pl.when(place(way) > 0)
            def _():
                run_copy(way, chip, piece).wait_recv()
                for p in pieces:
                    more = run_in[way, chip, p, rows, :].astype(F32)
                    if piece < PIECES:
                        gq_ref[2 * p : 2 * p + 2] += more.T.reshape(2, 128, 128)
                    else:
                        gkv_ref[2 * p] += more[:, 0:128]
                        gkv_ref[2 * p + 1] += more[:, 128:256]

    def drain(at, carry):
        for piece in range(PIECES + 1):
            for way in range(2):
                @pl.when((place(way) < LAST) & ((at <= chip) if way == 0 else (at >= chip)))
                def _():
                    ag_copy(at, piece, sibling, ag_s.at[way, at, piece]).wait_send()

                @pl.when((at > chip) if way == 0 else (at < chip))
                def _():
                    run_copy(way, at, piece).wait_send()
            ag_copy(at, piece, sibling, ag_s.at[2, at, piece]).wait_send()
            sib_copy(at, piece).wait_send()
        return carry

    lax.fori_loop(0, CHIPS, drain, 0)


def per_device(tokens, context_gradient, query_codes, query_scale, keyval_codes, keyval_scale):
    seq_count, length, width = tokens.shape
    tok_count = seq_count * length
    dma = pltpu.SemaphoreType.DMA
    vmem = pl.BlockSpec(memory_space=pltpu.VMEM)
    out = pl.pallas_call(
        kernel,
        out_shape=(
            jax.ShapeDtypeStruct((tok_count, 128), BF16),
            jax.ShapeDtypeStruct((6, 128, 128), F32),
            jax.ShapeDtypeStruct((6, 32, 128), F32),
        ),
        in_specs=[pl.BlockSpec(memory_space=pltpu.HBM)] * 6,
        out_specs=(vmem, vmem, vmem),
        scratch_shapes=[
            pltpu.VMEM((tok_count, 128), BF16),
            pltpu.VMEM((6, 128, 128), BF16),
            pltpu.VMEM((6, 128), BF16),
            pltpu.VMEM((6, 32, 128), BF16),
            pltpu.VMEM((6, 32), BF16),
            pltpu.VMEM((36, tok_count, STEP), BF16),
            pltpu.VMEM((12, 768, 128), BF16),
            pltpu.VMEM((12, 32, 768), BF16),
            pltpu.VMEM((GROUP, 2, 16, tok_count), BF16),
            pltpu.VMEM((tok_count, 128), F32),
            pltpu.VMEM((32, tok_count), F32),
            pltpu.VMEM((160, tok_count), BF16),
            pltpu.VMEM((GROUP, 2, 16, tok_count), F32),
            pltpu.VMEM((GROUP, 2, 16, tok_count), BF16),
            pltpu.VMEM((3, 2, 2, 16, tok_count), BF16),
            pltpu.VMEM((2, 2, 16, tok_count), F32),
            pltpu.VMEM((2, 16, tok_count), BF16),
            pltpu.VMEM((2, 16, tok_count), BF16),
            pltpu.VMEM((tok_count, length), F32),
            pltpu.VMEM((tok_count, 128), BF16),
            pltpu.VMEM((tok_count, length), BF16),
            pltpu.VMEM((tok_count, length), BF16),
            pltpu.VMEM((CHIPS, PIECES, 160, STEP), BF16),
            pltpu.VMEM((CHIPS, PIECES, 160, STEP), BF16),
            pltpu.VMEM((CHIPS, PIECES, 160, STEP), BF16),
            pltpu.VMEM((CHIPS, PIECES, 160, STEP), BF16),
            pltpu.VMEM((2, CHIPS, PIECES, 160, STEP), BF16),
            dma((5,)),
            dma(()),
            dma((12, PIECES + 1)),
            dma((3, CHIPS, PIECES + 1)),
            dma((2, CHIPS, PIECES + 1)),
            dma((CHIPS, PIECES + 1)),
            dma((CHIPS, PIECES + 1)),
            dma((CHIPS, PIECES + 1)),
            dma((2,)),
            dma((3,)),
            dma((3,)),
            dma((2,)),
            dma((3,)),
            dma((3,)),
        ],
        compiler_params=pltpu.CompilerParams(
            collective_id=0, has_side_effects=True, vmem_limit_bytes=VLIM * 1024 * 1024
        ),
    )(
        tokens.reshape(tok_count, width),
        context_gradient.reshape(tok_count, 128),
        query_codes,
        query_scale,
        keyval_codes.transpose(0, 2, 1),
        keyval_scale,
    )
    return out[0].reshape(context_gradient.shape), out[1], out[2].transpose(0, 2, 1)


def solution(mesh):
    return jax.shard_map(
        per_device,
        mesh=mesh,
        in_specs=(
            P("dp", None, None),
            P("dp", None, "node"),
            P("dp", None, "node"),
            P("dp", "node"),
            P("dp", None, "node"),
            P("dp", "node"),
        ),
        out_specs=(P("dp", None, "node"), P("dp", None, "node"), P("dp", None, "node")),
        check_vma=False,
    )
```

```python
import functools
import math

import jax
import jax.numpy as jnp
from jax import lax
from jax.experimental import pallas as pl
from jax.experimental.pallas import tpu as pltpu
from jax.sharding import PartitionSpec as P

MESH = pl.DeviceIdType.MESH
F32 = jnp.float32
BF16 = jnp.bfloat16
CHIPS = 6
LAST = CHIPS - 1
PIECES = 3
STEP = 256
GROUP = 8
VLIM = 60
KV_LAG, Q_LAG, Z_SLOTS = 1, 3, 3


def dot(a, b, dim_a=1, dim_b=0):
    return lax.dot_general(a, b, (((dim_a,), (dim_b,)), ((), ())), preferred_element_type=F32)


def kernel(
    tok_hbm, grad_hbm, qc_hbm, qs_hbm, kc_hbm, ks_hbm,
    ctx_ref, gq_ref, gkv_ref,
    grad_ref, qc_ref, qs_ref, kc_ref, ks_ref, x_all, wq, wkv, kv, q_acc, kv_acc, back, kv_part, kv_low, kv_in, pair_sum, z_out, z_in,
    grad_values, q_low, attend_low, scores_low, own_part, sib_out, sib_in, run_out, run_in,
    kv_own, kv_sib_out, kv_sib_in, kv_run_out, kv_run_in, kv_total,
    kv_s, kv_r,
    in_sem, x_sem, ag_r, ag_s, rs_r, rs_s, sib_r, sib_s, kvz, kvx_s, kvx_r, dkz, dkx_s, dkx_r,
):
    dp = lax.axis_index("dp")
    node = lax.axis_index("node")
    chip = dp // 2
    core = dp % 2
    member = node % GROUP
    z_hi = member % 2
    x_at = member // 2
    sibling = {"dp": 2 * chip + 1 - core}
    z_twin = {"node": node + 1 - 2 * z_hi}
    tok_count = grad_ref.shape[0]
    length = scores_low.shape[1]

    def x_mate(delta):
        return {"node": node - member + ((x_at + delta) % 4) * 2 + z_hi}

    def place(way):
        return chip if way == 0 else LAST - chip

    def ahead(way):
        return {"dp": dp + 2 if way == 0 else dp - 2}

    def chip_of(way, position):
        return position if way == 0 else LAST - position

    def remote(src, dst, s_sem, r_sem, to):
        return pltpu.make_async_remote_copy(
            src_ref=src, dst_ref=dst, send_sem=s_sem, recv_sem=r_sem, device_id=to, device_id_type=MESH
        )

    small = [
        pltpu.make_async_copy(src, dst, in_sem.at[i])
        for i, (src, dst) in enumerate(
            ((kc_hbm, kc_ref), (ks_hbm, ks_ref), (qc_hbm, qc_ref), (qs_hbm, qs_ref), (grad_hbm, grad_ref))
        )
    ]
    for copy in small:
        copy.start()
    loaded = x_all.at[pl.ds(0, 32)]
    x_copy = pltpu.make_async_copy(loaded, loaded, x_sem)

    barrier = pltpu.get_barrier_semaphore()
    others = [(chip + i) % CHIPS for i in range(1, CHIPS)]
    partners = [sibling, z_twin, x_mate(1), x_mate(2), x_mate(3)] + [{"dp": 2 * other + core} for other in others]
    for to in partners:
        pl.semaphore_signal(barrier, inc=1, device_id=to, device_id_type=MESH)

    for copy in small:
        copy.wait()
    diagonal = lax.broadcasted_iota(jnp.int32, (32, 32), 0) == lax.broadcasted_iota(jnp.int32, (32, 32), 1)
    for b in range(6):
        rows = pl.ds(b * 128, 128)
        scale = jnp.where(diagonal, ks_ref[b : b + 1, :].astype(F32), 0.0).sum(axis=1, keepdims=True)
        wkv[dp, :, rows] = (kc_ref[b].astype(F32) * scale).astype(BF16)
    for b in range(6):
        rows = pl.ds(b * 128, 128)
        wq[dp, rows, :] = (qc_ref[b].astype(F32) * qs_ref[b : b + 1, :].astype(F32)).astype(BF16)
    pl.semaphore_wait(barrier, len(partners))

    def chunk(owner, piece):
        if isinstance(piece, int) and piece == 0:
            return wkv.at[owner]
        return wq.at[owner, pl.ds(pl.multiple_of((piece - 1) * STEP, STEP), STEP), :]

    def ag_copy(src_chip, piece, to, s_sem):
        owner = 2 * src_chip + core
        part = chunk(owner, piece)
        return remote(part, part, s_sem, ag_r.at[owner, piece], to)

    def ag_wait(owner, piece):
        part = chunk(owner, piece)
        remote(part, part, ag_s.at[2, 0, piece], ag_r.at[owner, piece], sibling).wait_recv()

    def ag_send(src_chip, piece, only=(0, 1)):
        for way in only:
            @pl.when(place(way) < LAST)
            def _():
                ag_copy(src_chip, piece, ahead(way), ag_s.at[way, src_chip, piece]).start()
        ag_copy(src_chip, piece, sibling, ag_s.at[2, src_chip, piece]).start()

    def use_kv(owner):
        total = kv_acc[...]
        for p in range(PIECES):
            total += dot(wkv[owner, :, p * STEP : (p + 1) * STEP], x_all[owner * PIECES + p], 1, 1)
        kv_acc[...] = total

    def use_q(owner, other, p):
        q_acc[...] += dot(x_all[owner * PIECES + p], wq[owner, p * STEP : (p + 1) * STEP, :]) + dot(
            x_all[other * PIECES + p], wq[other, p * STEP : (p + 1) * STEP, :]
        )

    def each_source(distance, body):
        for way in range(2):
            src = chip_of(way, place(way) - distance)
            @pl.when(place(way) >= distance)
            def _():
                body(way, src)

    def take(src, piece):
        other = 2 * src + 1 - core
        ag_wait(other, piece)
        if piece == 0:
            use_kv(2 * src + core)
            use_kv(other)
        else:
            use_q(2 * src + core, other, piece - 1)

    q_acc[...] = jnp.zeros_like(q_acc)
    kv_acc[...] = jnp.zeros_like(kv_acc)
    def pass_on(distance, piece):
        def body(way, src):
            ag_wait(2 * src + core, piece)
            ag_send(src, piece, (way,))
        each_source(distance, body)

    order = [(0,0),(1,0),(2,0),(0,1),(3,0),(1,1),(0,2),(2,1),(3,1),(0,3),(1,2),(2,2),(0,4),(3,2),(1,3),(0,5),(2,3),(3,3)] + [(p, d) for d in (4, 5) for p in (1, 2, 3)]

    def pass_slot(piece, distance):
        if distance == 0:
            ag_send(chip, piece)
        else:
            pass_on(distance, piece)

    def use_slot(piece, distance):
        if distance == 0:
            take(chip, piece)
        else:
            each_source(distance, lambda way, src: take(src, piece))

    pair = pl.ds(x_at * 2, 2)
    z_copy = remote(kv.at[member], kv.at[member], kvz.at[0], kvz.at[1], z_twin)
    kv_copies = [
        remote(kv.at[pair], kv.at[pair], kvx_s.at[delta - 1], kvx_r.at[delta - 1], x_mate(delta))
        for delta in (1, 2, 3)
    ]
    waiting = []
    since_kv = None
    for at, slot in enumerate(order):
        pass_slot(*slot)
        if at == 0:
            for i in range(32):
                pltpu.make_async_copy(tok_hbm.at[:, pl.ds(i * STEP, STEP)], x_all.at[i], x_sem).start()
        if at == 3:
            x_all[32:36] = jnp.zeros((4, tok_count, STEP), BF16)
            x_copy.wait()
        waiting.append((at + (KV_LAG if slot[0] == 0 else Q_LAG), slot))
        if at >= 3:
            for due, ready in [w for w in waiting if w[0] <= at]:
                use_slot(*ready)
                waiting.remove((due, ready))
                if ready == (0, LAST):
                    kv[member] = kv_acc[...].astype(BF16).reshape(2, 16, tok_count)
                    z_copy.start()
                    since_kv = at
        if since_kv is not None and at == since_kv + Z_SLOTS:
            z_copy.wait()
            for copy in kv_copies:
                copy.start()
    last = waiting.pop()
    for due, ready in waiting:
        use_slot(*ready)
    for copy in kv_copies:
        copy.wait()
    for s in range(tok_count // length):
        at = slice(s * length, (s + 1) * length)
        grad_values[at, :] = dot(grad_ref[at, :], kv[:, 1, :, at].reshape(128, length))
    use_slot(*last[1])

    factor = 1.0 / math.sqrt(128)
    keys = kv[:, 0].reshape(128, tok_count)
    values = kv[:, 1].reshape(128, tok_count)
    seen = lax.broadcasted_iota(jnp.int32, (length, length), 0) >= lax.broadcasted_iota(
        jnp.int32, (length, length), 1
    )
    for s in range(tok_count // length):
        at = slice(s * length, (s + 1) * length)
        queries = q_acc[at, :].astype(BF16)
        q_low[at, :] = queries
        scores = jnp.where(seen, dot(queries, keys[:, at]) * factor, -jnp.inf)
        shifted = jnp.exp(scores - jnp.max(scores, axis=1, keepdims=True))
        attend = shifted / jnp.sum(shifted, axis=1, keepdims=True)
        attend_low[at, :] = attend.astype(BF16)
        back_attend = grad_values[at, :]
        center = jnp.sum(back_attend * attend, axis=1, keepdims=True)
        back_scores = (attend * (back_attend - center) * factor).astype(BF16)
        scores_low[at, :] = back_scores
        back[0:128, at] = dot(keys[:, at], back_scores, 1, 1).astype(BF16)

    def rest_of_attention():
        for s in range(tok_count // length):
            at = slice(s * length, (s + 1) * length)
            kv_part[:, 0, :, at] = dot(q_low[at, :], scores_low[at, :], 0, 0).reshape(GROUP, 16, length)
            kv_part[:, 1, :, at] = dot(grad_ref[at, :], attend_low[at, :], 0, 0).reshape(GROUP, 16, length)
        kv_low[...] = kv_part[...].astype(BF16)
        for copy in dk_copies:
            copy.start()
        for s in range(tok_count // length):
            at = slice(s * length, (s + 1) * length)
            ctx_ref[at, :] = dot(attend_low[at, :], values[:, at], 1, 1).astype(BF16)

    dk_copies = []
    for delta in (1, 2, 3):
        theirs = pl.ds(((x_at + delta) % 4) * 2, 2)
        dk_copies.append(
            remote(kv_low.at[theirs], kv_in.at[delta - 1], dkx_s.at[delta - 1], dkx_r.at[delta - 1], x_mate(delta))
        )

    def sib_copy(dest, piece):
        if piece < PIECES:
            src, dst = sib_out.at[dest, piece], sib_in.at[dest, piece]
        else:
            src, dst = kv_sib_out.at[dest], kv_sib_in.at[dest]
        return remote(src, dst, sib_s.at[dest, piece], sib_r.at[dest, piece], sibling)

    def run_copy(way, dest, p):
        src, dst = run_out.at[dest, p], run_in.at[way, dest, p]
        return remote(src, dst, rs_s.at[dest, p], rs_r.at[way, dest, p], ahead(way))

    q_rows, kv_rows = slice(0, 128), slice(128, 160)

    def terms(dest, rows):
        own_to, sib_to = (own_part, sib_out) if rows == q_rows else (kv_own, kv_sib_out)
        theirs = (2 * dest + 1 - core) * PIECES
        ours = (2 * dest + core) * PIECES
        low = back[rows, :]
        sib = [dot(low, x_all[theirs + p]).astype(BF16) for p in range(PIECES)]
        own = [dot(low, x_all[ours + p]).astype(BF16) for p in range(PIECES)]
        for p in range(PIECES):
            sib_to[dest, p] = sib[p]
        for piece in range(PIECES) if rows == q_rows else (PIECES,):
            sib_copy(dest, piece).start()
        for p in range(PIECES):
            own_to[dest, p] = own[p]

    def each_dest(time, body):
        for way in range(2):
            dest = chip_of(way, LAST - time + place(way))
            @pl.when(time >= place(way))
            def _():
                body(way, dest)

    def combine(way, dest, p):
        sib_copy(dest, p).wait_recv()

        @pl.when(place(way) > 0)
        def _():
            run_copy(way, dest, p).wait_recv()
            run_out[dest, p] = (
                own_part[dest, p].astype(F32) + sib_in[dest, p].astype(F32) + run_in[way, dest, p].astype(F32)
            ).astype(BF16)

        @pl.when(place(way) == 0)
        def _():
            run_out[dest, p] = (own_part[dest, p].astype(F32) + sib_in[dest, p].astype(F32)).astype(BF16)

        run_copy(way, dest, p).start()

    def q_terms(time):
        each_dest(time, lambda way, dest: terms(dest, q_rows))

    def q_combine(time, p):
        each_dest(time, lambda way, dest: combine(way, dest, p))

    TURN = 2

    def kv_copy(way, dest, straight):
        slot = 2 * CHIPS + chip if straight else way * CHIPS + dest
        to = {"dp": 2 * dest + core} if straight else ahead(way)
        return remote(kv_run_out.at[dest], kv_run_in.at[slot], kv_s.at[dest], kv_r.at[slot], to)

    def kv_arrived(slot):
        part = kv_run_in.at[slot]
        remote(part, part, kv_s.at[0], kv_r.at[slot], sibling).wait_recv()

    def each_kv(time, body):
        for way in range(2):
            at = place(way)
            base = at * (at <= TURN).astype(jnp.int32)
            dest_at = LAST - time + base
            @pl.when((time >= base) & (dest_at > at))
            def _():
                body(way, at, chip_of(way, dest_at))

    def kv_terms(time):
        each_kv(time, lambda way, at, dest: terms(dest, kv_rows))

    def kv_send(time):
        def body(way, at, dest):
            sib_copy(dest, PIECES).wait_recv()
            inner = (at > 0) & (at <= TURN)

            @pl.when(inner)
            def _():
                kv_arrived(way * CHIPS + dest)
                kv_run_out[dest] = (
                    kv_own[dest].astype(F32)
                    + kv_sib_in[dest].astype(F32)
                    + kv_run_in[way * CHIPS + dest].astype(F32)
                ).astype(BF16)

            @pl.when(jnp.logical_not(inner))
            def _():
                kv_run_out[dest] = (kv_own[dest].astype(F32) + kv_sib_in[dest].astype(F32)).astype(BF16)

            @pl.when(at < TURN)
            def _():
                kv_copy(way, dest, False).start()

            @pl.when(at >= TURN)
            def _():
                kv_copy(way, dest, True).start()

        each_kv(time, body)

    def q_time(time):
        q_terms(time)
        for p in range(PIECES):
            q_combine(time, p)

    q_time(0)
    rest_of_attention()
    q_time(1)

    for copy in dk_copies:
        copy.wait()
    pair_sum[...] = (
        kv_part[pair] + kv_in[0].astype(F32) + kv_in[1].astype(F32) + kv_in[2].astype(F32)
    )
    z_out[...] = pair_sum[1 - z_hi].astype(BF16)
    dz_copy = remote(z_out, z_in, dkz.at[0], dkz.at[1], z_twin)
    dz_copy.start()
    q_time(2)
    q_terms(3)
    q_combine(3, 0)
    q_combine(3, 1)
    dz_copy.wait()
    back[128:160, :] = (pair_sum[z_hi] + z_in[...].astype(F32)).astype(BF16).reshape(32, tok_count)
    kv_terms(0)
    kv_terms(1)
    kv_send(0)
    q_combine(3, 2)
    kv_terms(2)
    kv_send(1)
    q_terms(4)
    q_combine(4, 0)
    kv_terms(3)
    kv_send(2)
    q_combine(4, 1)
    kv_terms(4)
    kv_send(3)
    terms(chip, q_rows)
    q_combine(4, 2)
    terms(chip, kv_rows)
    kv_send(4)

    for p in range(PIECES):
        sib_copy(chip, p).wait_recv()
        gq_ref[2 * p : 2 * p + 2] = (
            (own_part[chip, p].astype(F32) + sib_in[chip, p].astype(F32)).T.reshape(2, 128, 128)
        )
        for way in range(2):
            @pl.when(place(way) > 0)
            def _():
                run_copy(way, chip, p).wait_recv()
                gq_ref[2 * p : 2 * p + 2] += run_in[way, chip, p].astype(F32).T.reshape(2, 128, 128)
    sib_copy(chip, PIECES).wait_recv()
    kv_total[...] = kv_own[chip].astype(F32) + kv_sib_in[chip].astype(F32)
    for way in range(2):
        @pl.when((place(way) > 0) & (place(way) <= TURN))
        def _():
            kv_arrived(way * CHIPS + chip)
            kv_total[...] += kv_run_in[way * CHIPS + chip].astype(F32)

        for at in range(TURN, LAST):
            @pl.when(place(way) > at)
            def _():
                kv_arrived(2 * CHIPS + chip_of(way, at))
                kv_total[...] += kv_run_in[2 * CHIPS + chip_of(way, at)].astype(F32)
    for b in range(6):
        gkv_ref[b] = kv_total[b // 2, :, (b % 2) * 128 : (b % 2 + 1) * 128]

    for other in others:
        kv_copy(0, other, True).wait_send()

    def drain(at, carry):
        for piece in range(PIECES + 1):
            for way in range(2):
                @pl.when((place(way) < LAST) & ((at <= chip) if way == 0 else (at >= chip)))
                def _():
                    ag_copy(at, piece, sibling, ag_s.at[way, at, piece]).wait_send()

                if piece < PIECES:
                    @pl.when((at > chip) if way == 0 else (at < chip))
                    def _():
                        run_copy(way, at, piece).wait_send()
            ag_copy(at, piece, sibling, ag_s.at[2, at, piece]).wait_send()
            sib_copy(at, piece).wait_send()
        return carry

    lax.fori_loop(0, CHIPS, drain, 0)


def per_device(tokens, context_gradient, query_codes, query_scale, keyval_codes, keyval_scale):
    seq_count, length, width = tokens.shape
    tok_count = seq_count * length
    dma = pltpu.SemaphoreType.DMA
    vmem = pl.BlockSpec(memory_space=pltpu.VMEM)
    out = pl.pallas_call(
        kernel,
        out_shape=(
            jax.ShapeDtypeStruct((tok_count, 128), BF16),
            jax.ShapeDtypeStruct((6, 128, 128), F32),
            jax.ShapeDtypeStruct((6, 32, 128), F32),
        ),
        in_specs=[pl.BlockSpec(memory_space=pltpu.HBM)] * 6,
        out_specs=(vmem, vmem, vmem),
        scratch_shapes=[
            pltpu.VMEM((tok_count, 128), BF16),
            pltpu.VMEM((6, 128, 128), BF16),
            pltpu.VMEM((6, 128), BF16),
            pltpu.VMEM((6, 32, 128), BF16),
            pltpu.VMEM((6, 32), BF16),
            pltpu.VMEM((36, tok_count, STEP), BF16),
            pltpu.VMEM((12, 768, 128), BF16),
            pltpu.VMEM((12, 32, 768), BF16),
            pltpu.VMEM((GROUP, 2, 16, tok_count), BF16),
            pltpu.VMEM((tok_count, 128), F32),
            pltpu.VMEM((32, tok_count), F32),
            pltpu.VMEM((160, tok_count), BF16),
            pltpu.VMEM((GROUP, 2, 16, tok_count), F32),
            pltpu.VMEM((GROUP, 2, 16, tok_count), BF16),
            pltpu.VMEM((3, 2, 2, 16, tok_count), BF16),
            pltpu.VMEM((2, 2, 16, tok_count), F32),
            pltpu.VMEM((2, 16, tok_count), BF16),
            pltpu.VMEM((2, 16, tok_count), BF16),
            pltpu.VMEM((tok_count, length), F32),
            pltpu.VMEM((tok_count, 128), BF16),
            pltpu.VMEM((tok_count, length), BF16),
            pltpu.VMEM((tok_count, length), BF16),
            pltpu.VMEM((CHIPS, PIECES, 128, STEP), BF16),
            pltpu.VMEM((CHIPS, PIECES, 128, STEP), BF16),
            pltpu.VMEM((CHIPS, PIECES, 128, STEP), BF16),
            pltpu.VMEM((CHIPS, PIECES, 128, STEP), BF16),
            pltpu.VMEM((2, CHIPS, PIECES, 128, STEP), BF16),
            pltpu.VMEM((CHIPS, PIECES, 32, STEP), BF16),
            pltpu.VMEM((CHIPS, PIECES, 32, STEP), BF16),
            pltpu.VMEM((CHIPS, PIECES, 32, STEP), BF16),
            pltpu.VMEM((CHIPS, PIECES, 32, STEP), BF16),
            pltpu.VMEM((3 * CHIPS, PIECES, 32, STEP), BF16),
            pltpu.VMEM((PIECES, 32, STEP), F32),
            dma((CHIPS,)),
            dma((3 * CHIPS,)),
            dma((5,)),
            dma(()),
            dma((12, PIECES + 1)),
            dma((3, CHIPS, PIECES + 1)),
            dma((2, CHIPS, PIECES)),
            dma((CHIPS, PIECES)),
            dma((CHIPS, PIECES + 1)),
            dma((CHIPS, PIECES + 1)),
            dma((2,)),
            dma((3,)),
            dma((3,)),
            dma((2,)),
            dma((3,)),
            dma((3,)),
        ],
        compiler_params=pltpu.CompilerParams(
            collective_id=0, has_side_effects=True, vmem_limit_bytes=VLIM * 1024 * 1024
        ),
    )(
        tokens.reshape(tok_count, width),
        context_gradient.reshape(tok_count, 128),
        query_codes,
        query_scale,
        keyval_codes.transpose(0, 2, 1),
        keyval_scale,
    )
    return out[0].reshape(context_gradient.shape), out[1], out[2].transpose(0, 2, 1)


def solution(mesh):
    return jax.shard_map(
        per_device,
        mesh=mesh,
        in_specs=(
            P("dp", None, None),
            P("dp", None, "node"),
            P("dp", None, "node"),
            P("dp", "node"),
            P("dp", None, "node"),
            P("dp", "node"),
        ),
        out_specs=(P("dp", None, "node"), P("dp", None, "node"), P("dp", None, "node")),
        check_vma=False,
    )
```

```python
import functools
import math

import jax
import jax.numpy as jnp
from jax import lax
from jax.experimental import pallas as pl
from jax.experimental.pallas import tpu as pltpu
from jax.sharding import PartitionSpec as P

MESH = pl.DeviceIdType.MESH
F32 = jnp.float32
BF16 = jnp.bfloat16
CHIPS = 6
LAST = CHIPS - 1
PIECES = 3
STEP = 256
GROUP = 8
VLIM = 60
KV_LAG, Q_LAG, Z_SLOTS = 1, 3, 3


def dot(a, b, dim_a=1, dim_b=0):
    return lax.dot_general(a, b, (((dim_a,), (dim_b,)), ((), ())), preferred_element_type=F32)


def kernel(
    tok_hbm, grad_hbm, qc_hbm, qs_hbm, kc_hbm, ks_hbm,
    ctx_ref, gq_ref, gkv_ref,
    grad_ref, qc_ref, qs_ref, kc_ref, ks_ref, x_all, wq, wkv, kv, q_acc, kv_acc, back, kv_part, kv_low, kv_in, pair_sum, z_out, z_in,
    grad_values, q_low, attend_low, scores_low, own_part, sib_out, sib_in, run_out, run_in,
    kv_own, kv_sib_out, kv_sib_in, kv_run_out, kv_run_in, kv_total,
    kv_s, kv_r,
    in_sem, x_sem, ag_r, ag_s, rs_r, rs_s, sib_r, sib_s, kvz, kvx_s, kvx_r, dkz, dkx_s, dkx_r,
):
    dp = lax.axis_index("dp")
    node = lax.axis_index("node")
    chip = dp // 2
    core = dp % 2
    member = node % GROUP
    z_hi = member % 2
    x_at = member // 2
    sibling = {"dp": 2 * chip + 1 - core}
    z_twin = {"node": node + 1 - 2 * z_hi}
    tok_count = grad_ref.shape[0]
    length = scores_low.shape[1]

    def x_mate(delta):
        return {"node": node - member + ((x_at + delta) % 4) * 2 + z_hi}

    def place(way):
        return chip if way == 0 else LAST - chip

    def ahead(way):
        return {"dp": dp + 2 if way == 0 else dp - 2}

    def chip_of(way, position):
        return position if way == 0 else LAST - position

    def remote(src, dst, s_sem, r_sem, to):
        return pltpu.make_async_remote_copy(
            src_ref=src, dst_ref=dst, send_sem=s_sem, recv_sem=r_sem, device_id=to, device_id_type=MESH
        )

    small = [
        pltpu.make_async_copy(src, dst, in_sem.at[i])
        for i, (src, dst) in enumerate(
            ((kc_hbm, kc_ref), (ks_hbm, ks_ref), (qc_hbm, qc_ref), (qs_hbm, qs_ref), (grad_hbm, grad_ref))
        )
    ]
    for copy in small:
        copy.start()
    loaded = x_all.at[pl.ds(0, 32)]
    x_copy = pltpu.make_async_copy(loaded, loaded, x_sem)

    barrier = pltpu.get_barrier_semaphore()
    others = [(chip + i) % CHIPS for i in range(1, CHIPS)]
    partners = [sibling, z_twin, x_mate(1), x_mate(2), x_mate(3)] + [{"dp": 2 * other + core} for other in others]
    for to in partners:
        pl.semaphore_signal(barrier, inc=1, device_id=to, device_id_type=MESH)

    for copy in small:
        copy.wait()
    diagonal = lax.broadcasted_iota(jnp.int32, (32, 32), 0) == lax.broadcasted_iota(jnp.int32, (32, 32), 1)
    for b in range(6):
        rows = pl.ds(b * 128, 128)
        scale = jnp.where(diagonal, ks_ref[b : b + 1, :].astype(F32), 0.0).sum(axis=1, keepdims=True)
        wkv[dp, :, rows] = (kc_ref[b].astype(F32) * scale).astype(BF16)
    for b in range(6):
        rows = pl.ds(b * 128, 128)
        wq[dp, rows, :] = (qc_ref[b].astype(F32) * qs_ref[b : b + 1, :].astype(F32)).astype(BF16)
    pl.semaphore_wait(barrier, len(partners))

    def chunk(owner, piece):
        if isinstance(piece, int) and piece == 0:
            return wkv.at[owner]
        return wq.at[owner, pl.ds(pl.multiple_of((piece - 1) * STEP, STEP), STEP), :]

    def ag_copy(src_chip, piece, to, s_sem):
        owner = 2 * src_chip + core
        part = chunk(owner, piece)
        return remote(part, part, s_sem, ag_r.at[owner, piece], to)

    def ag_wait(owner, piece):
        part = chunk(owner, piece)
        remote(part, part, ag_s.at[2, 0, piece], ag_r.at[owner, piece], sibling).wait_recv()

    def ag_send(src_chip, piece, only=(0, 1)):
        for way in only:
            @pl.when(place(way) < LAST)
            def _():
                ag_copy(src_chip, piece, ahead(way), ag_s.at[way, src_chip, piece]).start()
        ag_copy(src_chip, piece, sibling, ag_s.at[2, src_chip, piece]).start()

    def use_kv(owner):
        total = kv_acc[...]
        for p in range(PIECES):
            total += dot(wkv[owner, :, p * STEP : (p + 1) * STEP], x_all[owner * PIECES + p], 1, 1)
        kv_acc[...] = total

    def use_q(owner, other, p):
        q_acc[...] += dot(x_all[owner * PIECES + p], wq[owner, p * STEP : (p + 1) * STEP, :]) + dot(
            x_all[other * PIECES + p], wq[other, p * STEP : (p + 1) * STEP, :]
        )

    def each_source(distance, body):
        for way in range(2):
            src = chip_of(way, place(way) - distance)
            @pl.when(place(way) >= distance)
            def _():
                body(way, src)

    def take(src, piece):
        other = 2 * src + 1 - core
        ag_wait(other, piece)
        if piece == 0:
            use_kv(2 * src + core)
            use_kv(other)
        else:
            use_q(2 * src + core, other, piece - 1)

    q_acc[...] = jnp.zeros_like(q_acc)
    kv_acc[...] = jnp.zeros_like(kv_acc)
    def pass_on(distance, piece):
        def body(way, src):
            ag_wait(2 * src + core, piece)
            ag_send(src, piece, (way,))
        each_source(distance, body)

    order = [(0,0),(1,0),(2,0),(0,1),(3,0),(1,1),(0,2),(2,1),(3,1),(0,3),(1,2),(2,2),(0,4),(3,2),(1,3),(0,5),(2,3),(3,3)] + [(p, d) for d in (4, 5) for p in (1, 2, 3)]

    def pass_slot(piece, distance):
        if distance == 0:
            ag_send(chip, piece)
        else:
            pass_on(distance, piece)

    def use_slot(piece, distance):
        if distance == 0:
            take(chip, piece)
        else:
            each_source(distance, lambda way, src: take(src, piece))

    pair = pl.ds(x_at * 2, 2)
    z_copy = remote(kv.at[member], kv.at[member], kvz.at[0], kvz.at[1], z_twin)
    kv_copies = [
        remote(kv.at[pair], kv.at[pair], kvx_s.at[delta - 1], kvx_r.at[delta - 1], x_mate(delta))
        for delta in (1, 2, 3)
    ]
    waiting = []
    since_kv = None
    for at, slot in enumerate(order):
        pass_slot(*slot)
        if at == 0:
            for i in range(32):
                pltpu.make_async_copy(tok_hbm.at[:, pl.ds(i * STEP, STEP)], x_all.at[i], x_sem).start()
        if at == 3:
            x_all[32:36] = jnp.zeros((4, tok_count, STEP), BF16)
            x_copy.wait()
        waiting.append((at + (KV_LAG if slot[0] == 0 else Q_LAG), slot))
        if at >= 3:
            for due, ready in [w for w in waiting if w[0] <= at]:
                use_slot(*ready)
                waiting.remove((due, ready))
                if ready == (0, LAST):
                    kv[member] = kv_acc[...].astype(BF16).reshape(2, 16, tok_count)
                    z_copy.start()
                    since_kv = at
        if since_kv is not None and at == since_kv + Z_SLOTS:
            z_copy.wait()
            for copy in kv_copies:
                copy.start()
    last = waiting.pop()
    for due, ready in waiting:
        use_slot(*ready)
    for copy in kv_copies:
        copy.wait()
    for s in range(tok_count // length):
        at = slice(s * length, (s + 1) * length)
        grad_values[at, :] = dot(grad_ref[at, :], kv[:, 1, :, at].reshape(128, length))
    use_slot(*last[1])

    factor = 1.0 / math.sqrt(128)
    keys = kv[:, 0].reshape(128, tok_count)
    values = kv[:, 1].reshape(128, tok_count)
    seen = lax.broadcasted_iota(jnp.int32, (length, length), 0) >= lax.broadcasted_iota(
        jnp.int32, (length, length), 1
    )
    for s in range(tok_count // length):
        at = slice(s * length, (s + 1) * length)
        queries = q_acc[at, :].astype(BF16)
        q_low[at, :] = queries
        scores = jnp.where(seen, dot(queries, keys[:, at]) * factor, -jnp.inf)
        shifted = jnp.exp(scores - jnp.max(scores, axis=1, keepdims=True))
        attend = shifted / jnp.sum(shifted, axis=1, keepdims=True)
        attend_low[at, :] = attend.astype(BF16)
        back_attend = grad_values[at, :]
        center = jnp.sum(back_attend * attend, axis=1, keepdims=True)
        back_scores = (attend * (back_attend - center) * factor).astype(BF16)
        scores_low[at, :] = back_scores
        back[0:128, at] = dot(keys[:, at], back_scores, 1, 1).astype(BF16)

    def rest_of_attention():
        for s in range(tok_count // length):
            at = slice(s * length, (s + 1) * length)
            kv_part[:, 0, :, at] = dot(q_low[at, :], scores_low[at, :], 0, 0).reshape(GROUP, 16, length)
            kv_part[:, 1, :, at] = dot(grad_ref[at, :], attend_low[at, :], 0, 0).reshape(GROUP, 16, length)
        kv_low[...] = kv_part[...].astype(BF16)
        for copy in dk_copies:
            copy.start()
        for s in range(tok_count // length):
            at = slice(s * length, (s + 1) * length)
            ctx_ref[at, :] = dot(attend_low[at, :], values[:, at], 1, 1).astype(BF16)

    dk_copies = []
    for delta in (1, 2, 3):
        theirs = pl.ds(((x_at + delta) % 4) * 2, 2)
        dk_copies.append(
            remote(kv_low.at[theirs], kv_in.at[delta - 1], dkx_s.at[delta - 1], dkx_r.at[delta - 1], x_mate(delta))
        )

    def sib_copy(dest, piece):
        if piece < PIECES:
            src, dst = sib_out.at[dest, piece], sib_in.at[dest, piece]
        else:
            src, dst = kv_sib_out.at[dest], kv_sib_in.at[dest]
        return remote(src, dst, sib_s.at[dest, piece], sib_r.at[dest, piece], sibling)

    def run_copy(way, dest, p):
        src, dst = run_out.at[dest, p], run_in.at[way, dest, p]
        return remote(src, dst, rs_s.at[dest, p], rs_r.at[way, dest, p], ahead(way))

    q_rows, kv_rows = slice(0, 128), slice(128, 160)

    def terms(dest, rows):
        own_to, sib_to = (own_part, sib_out) if rows == q_rows else (kv_own, kv_sib_out)
        theirs = (2 * dest + 1 - core) * PIECES
        ours = (2 * dest + core) * PIECES
        low = back[rows, :]
        sib = [dot(low, x_all[theirs + p]).astype(BF16) for p in range(PIECES)]
        own = [dot(low, x_all[ours + p]).astype(BF16) for p in range(PIECES)]
        for p in range(PIECES):
            sib_to[dest, p] = sib[p]
        for piece in range(PIECES) if rows == q_rows else (PIECES,):
            sib_copy(dest, piece).start()
        for p in range(PIECES):
            own_to[dest, p] = own[p]

    def each_dest(time, body):
        for way in range(2):
            dest = chip_of(way, LAST - time + place(way))
            @pl.when(time >= place(way))
            def _():
                body(way, dest)

    def combine(way, dest, p):
        sib_copy(dest, p).wait_recv()

        @pl.when(place(way) > 0)
        def _():
            run_copy(way, dest, p).wait_recv()
            run_out[dest, p] = (
                own_part[dest, p].astype(F32) + sib_in[dest, p].astype(F32) + run_in[way, dest, p].astype(F32)
            ).astype(BF16)

        @pl.when(place(way) == 0)
        def _():
            run_out[dest, p] = (own_part[dest, p].astype(F32) + sib_in[dest, p].astype(F32)).astype(BF16)

        run_copy(way, dest, p).start()

    def q_terms(time):
        each_dest(time, lambda way, dest: terms(dest, q_rows))

    def q_combine(time, p):
        each_dest(time, lambda way, dest: combine(way, dest, p))

    TURN = 1

    def kv_copy(way, dest, straight):
        slot = 2 * CHIPS + chip if straight else way * CHIPS + dest
        to = {"dp": 2 * dest + core} if straight else ahead(way)
        return remote(kv_run_out.at[dest], kv_run_in.at[slot], kv_s.at[dest], kv_r.at[slot], to)

    def kv_arrived(slot):
        part = kv_run_in.at[slot]
        remote(part, part, kv_s.at[0], kv_r.at[slot], sibling).wait_recv()

    def each_kv(time, body):
        for way in range(2):
            at = place(way)
            base = at * (at <= TURN).astype(jnp.int32)
            dest_at = LAST - time + base
            @pl.when((time >= base) & (dest_at > at))
            def _():
                body(way, at, chip_of(way, dest_at))

    def kv_terms(time):
        each_kv(time, lambda way, at, dest: terms(dest, kv_rows))

    def kv_send(time):
        def body(way, at, dest):
            sib_copy(dest, PIECES).wait_recv()
            inner = (at > 0) & (at <= TURN)

            @pl.when(inner)
            def _():
                kv_arrived(way * CHIPS + dest)
                kv_run_out[dest] = (
                    kv_own[dest].astype(F32)
                    + kv_sib_in[dest].astype(F32)
                    + kv_run_in[way * CHIPS + dest].astype(F32)
                ).astype(BF16)

            @pl.when(jnp.logical_not(inner))
            def _():
                kv_run_out[dest] = (kv_own[dest].astype(F32) + kv_sib_in[dest].astype(F32)).astype(BF16)

            @pl.when(at < TURN)
            def _():
                kv_copy(way, dest, False).start()

            @pl.when(at >= TURN)
            def _():
                kv_copy(way, dest, True).start()

        each_kv(time, body)

    def q_time(time):
        q_terms(time)
        for p in range(PIECES):
            q_combine(time, p)

    def first_terms(way, dest):
        for p in range(PIECES):
            sib_out[dest, p] = dot(back[q_rows, :], x_all[(2 * dest + 1 - core) * PIECES + p]).astype(BF16)
            sib_copy(dest, p).start()
        for p in range(PIECES):
            own_part[dest, p] = dot(back[q_rows, :], x_all[(2 * dest + core) * PIECES + p]).astype(BF16)

    each_dest(0, first_terms)
    for p in range(PIECES):
        q_combine(0, p)
    rest_of_attention()
    q_time(1)

    for copy in dk_copies:
        copy.wait()
    pair_sum[...] = (
        kv_part[pair] + kv_in[0].astype(F32) + kv_in[1].astype(F32) + kv_in[2].astype(F32)
    )
    z_out[...] = pair_sum[1 - z_hi].astype(BF16)
    dz_copy = remote(z_out, z_in, dkz.at[0], dkz.at[1], z_twin)
    dz_copy.start()
    q_time(2)
    q_terms(3)
    q_combine(3, 0)
    q_combine(3, 1)
    dz_copy.wait()
    back[128:160, :] = (pair_sum[z_hi] + z_in[...].astype(F32)).astype(BF16).reshape(32, tok_count)
    kv_terms(0)
    kv_terms(1)
    kv_send(0)
    q_combine(3, 2)
    kv_terms(2)
    kv_send(1)
    q_terms(4)
    q_combine(4, 0)
    kv_terms(3)
    kv_send(2)
    q_combine(4, 1)
    kv_terms(4)
    kv_send(3)
    terms(chip, q_rows)
    q_combine(4, 2)
    terms(chip, kv_rows)
    kv_send(4)

    def drain(at, carry):
        for way in range(2):
            @pl.when((place(way) < LAST) & ((at <= chip) if way == 0 else (at >= chip)))
            def _():
                for piece in range(PIECES + 1):
                    ag_copy(at, piece, sibling, ag_s.at[way, at, piece]).wait_send()
        for piece in range(PIECES + 1):
            ag_copy(at, piece, sibling, ag_s.at[2, at, piece]).wait_send()
            sib_copy(at, piece).wait_send()
        return carry

    lax.fori_loop(0, CHIPS, drain, 0)

    for p in range(PIECES):
        sib_copy(chip, p).wait_recv()
        gq_ref[2 * p : 2 * p + 2] = (
            (own_part[chip, p].astype(F32) + sib_in[chip, p].astype(F32)).T.reshape(2, 128, 128)
        )
        for way in range(2):
            @pl.when(place(way) > 0)
            def _():
                run_copy(way, chip, p).wait_recv()
                gq_ref[2 * p : 2 * p + 2] += run_in[way, chip, p].astype(F32).T.reshape(2, 128, 128)
    sib_copy(chip, PIECES).wait_recv()
    kv_total[...] = kv_own[chip].astype(F32) + kv_sib_in[chip].astype(F32)
    for way in range(2):
        @pl.when((place(way) > 0) & (place(way) <= TURN))
        def _():
            kv_arrived(way * CHIPS + chip)
            kv_total[...] += kv_run_in[way * CHIPS + chip].astype(F32)

        for at in range(TURN, LAST):
            @pl.when(place(way) > at)
            def _():
                kv_arrived(2 * CHIPS + chip_of(way, at))
                kv_total[...] += kv_run_in[2 * CHIPS + chip_of(way, at)].astype(F32)
    for b in range(6):
        gkv_ref[b] = kv_total[b // 2, :, (b % 2) * 128 : (b % 2 + 1) * 128]

    for other in others:
        kv_copy(0, other, True).wait_send()

    def drain_sums(at, carry):
        for way in range(2):
            @pl.when((at > chip) if way == 0 else (at < chip))
            def _():
                for p in range(PIECES):
                    run_copy(way, at, p).wait_send()
        return carry

    lax.fori_loop(0, CHIPS, drain_sums, 0)


def per_device(tokens, context_gradient, query_codes, query_scale, keyval_codes, keyval_scale):
    seq_count, length, width = tokens.shape
    tok_count = seq_count * length
    dma = pltpu.SemaphoreType.DMA
    vmem = pl.BlockSpec(memory_space=pltpu.VMEM)
    out = pl.pallas_call(
        kernel,
        out_shape=(
            jax.ShapeDtypeStruct((tok_count, 128), BF16),
            jax.ShapeDtypeStruct((6, 128, 128), F32),
            jax.ShapeDtypeStruct((6, 32, 128), F32),
        ),
        in_specs=[pl.BlockSpec(memory_space=pltpu.HBM)] * 6,
        out_specs=(vmem, vmem, vmem),
        scratch_shapes=[
            pltpu.VMEM((tok_count, 128), BF16),
            pltpu.VMEM((6, 128, 128), BF16),
            pltpu.VMEM((6, 128), BF16),
            pltpu.VMEM((6, 32, 128), BF16),
            pltpu.VMEM((6, 32), BF16),
            pltpu.VMEM((36, tok_count, STEP), BF16),
            pltpu.VMEM((12, 768, 128), BF16),
            pltpu.VMEM((12, 32, 768), BF16),
            pltpu.VMEM((GROUP, 2, 16, tok_count), BF16),
            pltpu.VMEM((tok_count, 128), F32),
            pltpu.VMEM((32, tok_count), F32),
            pltpu.VMEM((160, tok_count), BF16),
            pltpu.VMEM((GROUP, 2, 16, tok_count), F32),
            pltpu.VMEM((GROUP, 2, 16, tok_count), BF16),
            pltpu.VMEM((3, 2, 2, 16, tok_count), BF16),
            pltpu.VMEM((2, 2, 16, tok_count), F32),
            pltpu.VMEM((2, 16, tok_count), BF16),
            pltpu.VMEM((2, 16, tok_count), BF16),
            pltpu.VMEM((tok_count, length), F32),
            pltpu.VMEM((tok_count, 128), BF16),
            pltpu.VMEM((tok_count, length), BF16),
            pltpu.VMEM((tok_count, length), BF16),
            pltpu.VMEM((CHIPS, PIECES, 128, STEP), BF16),
            pltpu.VMEM((CHIPS, PIECES, 128, STEP), BF16),
            pltpu.VMEM((CHIPS, PIECES, 128, STEP), BF16),
            pltpu.VMEM((CHIPS, PIECES, 128, STEP), BF16),
            pltpu.VMEM((2, CHIPS, PIECES, 128, STEP), BF16),
            pltpu.VMEM((CHIPS, PIECES, 32, STEP), BF16),
            pltpu.VMEM((CHIPS, PIECES, 32, STEP), BF16),
            pltpu.VMEM((CHIPS, PIECES, 32, STEP), BF16),
            pltpu.VMEM((CHIPS, PIECES, 32, STEP), BF16),
            pltpu.VMEM((3 * CHIPS, PIECES, 32, STEP), BF16),
            pltpu.VMEM((PIECES, 32, STEP), F32),
            dma((CHIPS,)),
            dma((3 * CHIPS,)),
            dma((5,)),
            dma(()),
            dma((12, PIECES + 1)),
            dma((3, CHIPS, PIECES + 1)),
            dma((2, CHIPS, PIECES)),
            dma((CHIPS, PIECES)),
            dma((CHIPS, PIECES + 1)),
            dma((CHIPS, PIECES + 1)),
            dma((2,)),
            dma((3,)),
            dma((3,)),
            dma((2,)),
            dma((3,)),
            dma((3,)),
        ],
        compiler_params=pltpu.CompilerParams(
            collective_id=0, has_side_effects=True, vmem_limit_bytes=VLIM * 1024 * 1024
        ),
    )(
        tokens.reshape(tok_count, width),
        context_gradient.reshape(tok_count, 128),
        query_codes,
        query_scale,
        keyval_codes.transpose(0, 2, 1),
        keyval_scale,
    )
    return out[0].reshape(context_gradient.shape), out[1], out[2].transpose(0, 2, 1)


def solution(mesh):
    return jax.shard_map(
        per_device,
        mesh=mesh,
        in_specs=(
            P("dp", None, None),
            P("dp", None, "node"),
            P("dp", None, "node"),
            P("dp", "node"),
            P("dp", None, "node"),
            P("dp", "node"),
        ),
        out_specs=(P("dp", None, "node"), P("dp", None, "node"), P("dp", None, "node")),
        check_vma=False,
    )
```
